32 devices in a mesh: row: 4 (over z), col: 4 (over y, core), rep: 2 (over x).
Axes of the slice: x: 2, y: 2, z: 4, core: 2. Of those that a mesh axis runs over, the one named last changes fastest.
Arguments:
- hamiltonian: bfloat16 [2048, 2048], P('row', ('rep', 'col')), may hold values from -0.21875 to 0.21875
- density: bfloat16 [2048, 2048], P(('rep', 'row'), 'col'), may hold values from -6 to 6
- ham_pattern: int32 [32, 32], P('row', ('rep', 'col')), may hold values 0 or 1
- den_pattern: int32 [32, 32], P(('rep', 'row'), 'col'), may hold values 0 or 1
- tile_basis: bfloat16 [64, 16, 512], P(None, None, 'col'), may hold values from -0.75 to 0.75
- offsets: int32 [32], P(('row', 'rep')), may hold values from 0 to 31
Outputs:
- product: bfloat16 [2048, 2048], P(('row', 'rep'), 'col')
- grid_density: float32 [256, 512], P(('row', 'rep'), 'col')
The draws below stay inside these ranges and needn't reach their ends.
All inputs are finite; a program needn't handle non-finite values. No bound on the sum of `ham_pattern` or of `den_pattern` on one device may be relied on, other than what follows from the above.
Results may differ from the reference program's by a relative error of at most 0.0004.
Values may be sent and summed in bfloat16 or wider, within the bound.
A program may use at most 128 MiB of HBM per device.

```python
import math
import jax
import jax.numpy as jnp
from jax import lax

BLK = 64
SX = 32
TX = 16
NB = 32
ATOMS_DEV = 4
NXG = 256
PL = 512


def with_ends(array, rng, smallest, high):
    longest = array.shape.index(max(array.shape))
    spots = []
    for shift in (0, 1):
        where = [jax.random.randint(jax.random.fold_in(rng, axis), (), 0, length) for axis, length in enumerate(array.shape)]
        where[longest] = (where[longest] + shift) % array.shape[longest]
        spots.append(tuple(where))
    return array.at[spots[0]].set(smallest).at[spots[1]].set(high)


def level_of(stream_key, extent, shards, smallest, largest):
    loudness, own = 1.0, jax.random.fold_in(stream_key, 6)
    for dim, blocks in shards:
        draws = jnp.exp(jax.random.uniform(jax.random.fold_in(own, dim), (blocks,), jnp.float32, smallest / len(shards), largest / len(shards)))
        loudness = loudness * jnp.repeat(draws, extent[dim] // blocks).reshape([-1 if axis == dim else 1 for axis in range(len(extent))])
    return loudness


def centred(own_key, shape, scale, limit, pieces=(), kind=jnp.bfloat16):
    drawn = scale * jax.random.normal(own_key, shape, jnp.float32)
    if pieces:
        drawn = drawn * level_of(own_key, shape, pieces, -0.22, 0.18)
    return jnp.clip(drawn, -limit, limit).astype(kind)


def setup_inputs(seed: int = 0) -> dict:
    key_list = jax.random.split(jax.random.key(seed), 7)
    return {
        "hamiltonian": centred(key_list[0], (NB * BLK, NB * BLK), (NB * BLK // 3) ** -0.5, 0.21875, ((0, 4), (1, 8))),
        "density": centred(key_list[1], (NB * BLK, NB * BLK), 1.0, 6.0, ((0, 8), (1, 4))),
        "ham_pattern": with_ends((jax.random.randint(key_list[2], (NB, NB), 0, 3) < 1).astype(jnp.int32), jax.random.fold_in(key_list[2], 1), 0, 1),
        "den_pattern": with_ends((jax.random.randint(key_list[3], (NB, NB), 0, 3) < 1).astype(jnp.int32), jax.random.fold_in(key_list[3], 1), 0, 1),
        "tile_basis": centred(key_list[4], (BLK, TX, PL), BLK ** -0.5, 0.75, ((2, 4),)),
        "offsets": with_ends(jax.random.randint(key_list[5], (NB,), 0, SX), jax.random.fold_in(key_list[5], 1), 0, SX - 1).astype(jnp.int32),
    }


def expand(matrix, pattern):
    rows_b, cols_b = pattern.shape
    weight = pattern.astype(matrix.dtype)
    shaped = matrix.reshape(rows_b, BLK, cols_b, BLK) * weight[:, None, :, None]
    return shaped.reshape(matrix.shape)

def reference(hamiltonian, density, ham_pattern, den_pattern, tile_basis, offsets):
    ham = expand(hamiltonian, ham_pattern)
    dens = expand(density, den_pattern)
    full = jnp.dot(ham, dens, preferred_element_type=jnp.float32)
    charges = lax.optimization_barrier(jnp.sum(full, axis=1)) * (1.0 / math.sqrt(NB * BLK))
    amplitudes = charges.reshape(NB, BLK)
    tiles = jnp.einsum('am,mtp->atp', amplitudes, tile_basis.astype(jnp.float32), precision=lax.Precision.HIGHEST)
    slab = jnp.arange(NB, dtype=jnp.int32) // ATOMS_DEV
    first = slab * SX + offsets.astype(jnp.int32)
    planes = (first[:, None] + jnp.arange(TX, dtype=jnp.int32)[None, :]) % NXG
    onehot = (planes[:, :, None] == jnp.arange(NXG, dtype=jnp.int32)[None, None, :]).astype(jnp.float32)
    grid_density = jnp.einsum('atx,atp->xp', onehot, tiles, precision=lax.Precision.HIGHEST)
    return (full.astype(jnp.bfloat16), grid_density)
```

```python
import functools
import math

import jax
import jax.numpy as jnp
from jax import lax
from jax.experimental import pallas as pl
from jax.experimental.pallas import tpu as pltpu
from jax.sharding import PartitionSpec as P

MESH = pl.DeviceIdType.MESH
TX = 16
LANES = 128
F32 = jnp.float32
BF16 = jnp.bfloat16
NT = (((1,), (1,)), ((), ()))


def flipped(index, mask):
    bit = 1
    while bit <= mask:
        if mask & bit:
            index = index + bit - 2 * bit * ((index // bit) % 2)
        bit *= 2
    return index


def low_bit(mask):
    return mask & -mask


def mask_row(pattern, row, width):
    blocks = pattern.shape[1]
    lane = lax.broadcasted_iota(jnp.int32, (1, width), 1) // (width // blocks)
    values = jnp.zeros((1, width), jnp.int32)
    for block in range(blocks):
        values = jnp.where(lane == block, pattern[row, block], values)
    return values.astype(F32).astype(BF16)


def kernel(
    R, C, ham, den, hpat, dpat, basis, offsets, out, grid,
    hbuf, dbuf, psend, pown, precv, scol, srow, tbuf, trecv, chcol, tiles, ext, incoming,
    hs, hr, drs, drr, dls, dlr, xs, xr, cs, cr, ws, wr, ts, tr, gs, gr,
):
    r, c, p = lax.axis_index("row"), lax.axis_index("col"), lax.axis_index("rep")
    MR, KH = ham.shape
    KD, W = den.shape
    MH, Q, KHALF = MR // 2, W // LANES, C * KH
    atoms = offsets.shape[0]
    block = MH // atoms
    sx = grid.shape[0]
    slab, slabs = r * 2 + p, R * 2
    after, before = (slab + 1) % slabs, (slab + slabs - 1) % slabs
    next_id = {"row": after // 2, "rep": after % 2}
    last_id = {"row": before // 2, "rep": before % 2}
    peer = {"rep": 1 - p}

    barrier = pltpu.get_barrier_semaphore()
    friends = [{"col": (c + k) % C} for k in range(1, C)] + [{"row": (r + k) % R} for k in range(1, R)]
    friends += [peer, next_id, last_id]
    for friend in friends:
        pl.semaphore_signal(barrier, inc=1, device_id=friend, device_id_type=MESH)

    def remote(src, dst, send, recv, to):
        return pltpu.make_async_remote_copy(
            src_ref=src, dst_ref=dst, send_sem=send, recv_sem=recv, device_id=to, device_id_type=MESH
        )

    def den_rows(q, owner):
        return dbuf.at[q, pl.ds(pl.multiple_of(owner * KD, KD), KD), :]

    def to_right(q, d):
        rows = den_rows(q, (r - d + R) % R)
        return remote(rows, rows, drs.at[q, d], drr.at[q, d + 1], {"row": (r + 1) % R})

    def to_left(q, d):
        rows = den_rows(q, (r + d) % R)
        return remote(rows, rows, dls.at[q, d], dlr.at[q, d + 1], {"row": (r + R - 1) % R})

    def send_right(q, d):
        @pl.when(jnp.logical_and(r - d >= 0, r + 1 < R))
        def _():
            to_right(q, d).start()

    def send_left(q, d):
        @pl.when(jnp.logical_and(r + d < R, r >= 1))
        def _():
            to_left(q, d).start()

    def own(q):
        send_right(q, 0)
        send_left(q, 0)

    def arrive(q, d):
        @pl.when(r - d >= 0)
        def _():
            rows = den_rows(q, (r - d + R) % R)
            remote(rows, rows, drs.at[q, d], drr.at[q, d], {"row": (r + 1) % R}).wait_recv()

        if d < R - 1:
            send_right(q, d)

        @pl.when(r + d < R)
        def _():
            rows = den_rows(q, (r + d) % R)
            remote(rows, rows, dls.at[q, d], dlr.at[q, d], {"row": (r + R - 1) % R}).wait_recv()

        if d < R - 1:
            send_left(q, d)

    bits = [1 << k for k in range(C.bit_length() - 1)]

    def ham_copy(mask, bit):
        source = hbuf.at[flipped(c, mask)]
        return remote(source, source, hs.at[mask, bit.bit_length() - 1], hr.at[mask | bit], {"col": flipped(c, bit)})

    def ham_forward(mask):
        for bit in reversed(bits):
            if mask == 0 or bit < low_bit(mask):
                ham_copy(mask, bit).start()

    def ham_arrive():
        for mask in sorted(range(1, C), key=lambda m: (-low_bit(m), m)):
            source = hbuf.at[flipped(c, mask)]
            remote(source, source, hs.at[mask, 0], hr.at[mask], {"col": flipped(c, 1)}).wait_recv()
            ham_forward(mask)

    dmasks = [mask_row(dpat, a, W) for a in range(dpat.shape[0])]
    tall = KD // dpat.shape[0]

    def mask_den(q):
        for a, values in enumerate(dmasks):
            rows = pl.ds(pl.multiple_of(r * KD + a * tall, tall), tall)
            dbuf[q, rows, :] = den[a * tall : (a + 1) * tall, q * LANES : (q + 1) * LANES] * values[:, q * LANES : (q + 1) * LANES]

    for q in range(Q):
        mask_den(q)
    high = MR // hpat.shape[0]
    for a in range(hpat.shape[0]):
        hbuf[c, a * high : (a + 1) * high, :] = ham[a * high : (a + 1) * high, :] * mask_row(hpat, a, KH)

    pl.semaphore_wait(barrier, len(friends))
    own(0)
    ham_forward(0)

    ones = jnp.ones((16, LANES), BF16)
    mine = jnp.zeros((16, KD), F32)
    for q in range(Q):
        mine += lax.dot_general(ones, den_rows(q, r)[...], NT, preferred_element_type=F32)
    scol[c] = mine[:8]

    def col_copy(k):
        return remote(scol.at[c], scol.at[c], cs.at[k], cr.at[k], {"col": (c + k) % C})

    for k in range(1, C):
        col_copy(k).start()
    if Q > 1:
        own(1)

    def row_copy(k):
        return remote(srow.at[r], srow.at[r], ws.at[k], wr.at[k], {"row": (r + k) % R})

    def sums_over_col():
        for k in range(1, C):
            source = scol.at[(c - k + C) % C]
            remote(source, source, cs.at[k], cr.at[k], {"col": (c + k) % C}).wait_recv()
        total = scol[0]
        for k in range(1, C):
            total += scol[k]
        srow[r] = total
        for k in range(1, R):
            row_copy(k).start()

    def t_copy():
        return remote(tbuf.at[1 - p], trecv, ts, tr, peer)

    def row_sums():
        for k in range(1, R):
            source = srow.at[(r - k + R) % R]
            remote(source, source, ws.at[k], wr.at[k], {"row": (r + k) % R}).wait_recv()
        step = min(KD, KH)
        total = jnp.zeros((24, MR), F32)
        for k in range(0, KHALF, step):
            piece = srow[k // KD, :, k % KD : k % KD + step]
            high_part = piece.astype(BF16).astype(F32)
            rest = piece - high_part
            mid_part = rest.astype(BF16).astype(F32)
            parts = jnp.concatenate([high_part, mid_part, rest - mid_part], axis=0).astype(BF16)
            total += lax.dot_general(
                parts, hbuf[k // KH, :, k % KH : k % KH + step], NT, preferred_element_type=F32
            )
        total = total[:8] + total[8:16] + total[16:]
        tbuf[0] = total[:, :MH]
        tbuf[1] = total[:, MH:]
        t_copy().start()

    def g_copy():
        return remote(ext.at[pl.ds(sx, TX), :], incoming, gs, gr, next_id)

    def collocate():
        t_copy().wait_recv()
        charges = (tbuf[p, 0:1, :] + trecv[0:1, :]) * (1.0 / math.sqrt(KHALF * 2))
        chcol[...] = jnp.transpose(jnp.broadcast_to(charges, (LANES, MH)))

        def body(m, sums):
            values = basis[m].astype(F32)
            return tuple(s + values * chcol[pl.ds(a * block + m, 1), :] for a, s in enumerate(sums))

        zero = jnp.zeros((TX, grid.shape[1]), F32)
        sums = lax.fori_loop(0, block, body, (zero,) * atoms, unroll=4)
        for a in range(atoms):
            tiles[a * TX : (a + 1) * TX, :] = sums[a]
        place = lax.broadcasted_iota(jnp.int32, (1, atoms * TX), 1)
        first = jnp.zeros((1, atoms * TX), jnp.int32)
        for a in range(atoms):
            first = jnp.where(place // TX == a, offsets[a], first)
        plane = lax.broadcasted_iota(jnp.int32, (sx + TX, atoms * TX), 0)
        onehot = jnp.where(plane == first + place % TX, 1.0, 0.0).astype(F32)
        ext[...] = jnp.dot(onehot, tiles[...], precision=lax.Precision.HIGHEST, preferred_element_type=F32)
        g_copy().start()

    def finish_grid():
        g_copy().wait_recv()
        grid[...] = ext[:sx, :]
        grid[:TX, :] = ext[:TX, :] + incoming[...]

    def x_copy(q):
        return remote(psend.at[q], precv.at[q], xs.at[q], xr.at[q], peer)

    def half(q, which):
        rows = pl.ds(pl.multiple_of(which * MH, MH), MH)
        total = jnp.zeros((MH, LANES), F32)
        for j in range(C):
            total += jnp.dot(hbuf[j, rows, :], dbuf[q, j * KH : (j + 1) * KH, :], preferred_element_type=F32)
        return total

    def multiply(q):
        psend[q] = half(q, 1 - p)
        x_copy(q).start()
        pown[q] = half(q, p)

    def drain(q):
        x_copy(q).wait_recv()
        out[:, q * LANES : (q + 1) * LANES] = (pown[q] + precv[q]).astype(BF16)

    hooks = {
        (0, 1): [sums_over_col],
        (0, R - 1): [ham_arrive],
        (1, 1): [row_sums, lambda: multiply(0)],
        (1, R - 1): [lambda: multiply(1)],
        (2, 1): [collocate],
        (2, R - 1): [lambda: multiply(2), lambda: drain(0)],
        (3, 1): [finish_grid, lambda: drain(1)],
        (3, R - 1): [lambda: multiply(3), lambda: drain(2), lambda: drain(3)],
    }
    for q in range(Q):
        for d in range(1, R):
            arrive(q, d)
            if d == R - 1 and q + 2 < Q:
                own(q + 2)
            for hook in hooks.get((q, d), []):
                hook()

    for q in range(Q):
        x_copy(q).wait_send()
        for d in range(R - 1):
            @pl.when(jnp.logical_and(r - d >= 0, r + 1 < R))
            def _():
                to_right(q, d).wait_send()

            @pl.when(jnp.logical_and(r + d < R, r >= 1))
            def _():
                to_left(q, d).wait_send()

    for mask in range(C):
        for bit in bits:
            if mask == 0 or bit < low_bit(mask):
                ham_copy(mask, bit).wait_send()
    for k in range(1, C):
        col_copy(k).wait_send()
    for k in range(1, R):
        row_copy(k).wait_send()
    t_copy().wait_send()
    g_copy().wait_send()


def shards(R, C, hamiltonian, density, ham_pattern, den_pattern, tile_basis, offsets):
    MR, KH = hamiltonian.shape
    KD, W = density.shape
    MH, Q, KHALF = MR // 2, W // LANES, C * KH
    cells, atoms = tile_basis.shape[2], offsets.shape[0]
    sx = 32
    dma = pltpu.SemaphoreType.DMA
    vmem = pl.BlockSpec(memory_space=pltpu.VMEM)
    smem = pl.BlockSpec(memory_space=pltpu.SMEM)
    return pl.pallas_call(
        functools.partial(kernel, R, C),
        out_shape=(jax.ShapeDtypeStruct((MH, W), BF16), jax.ShapeDtypeStruct((sx, cells), F32)),
        in_specs=[vmem, vmem, smem, smem, vmem, smem],
        out_specs=(vmem, vmem),
        scratch_shapes=[
            pltpu.VMEM((C, MR, KH), BF16),
            pltpu.VMEM((Q, KHALF, LANES), BF16),
            pltpu.VMEM((Q, MH, LANES), F32),
            pltpu.VMEM((Q, MH, LANES), F32),
            pltpu.VMEM((Q, MH, LANES), F32),
            pltpu.VMEM((C, 8, KD), F32),
            pltpu.VMEM((R, 8, KD), F32),
            pltpu.VMEM((2, 8, MH), F32),
            pltpu.VMEM((8, MH), F32),
            pltpu.VMEM((MH, LANES), F32),
            pltpu.VMEM((atoms * TX, cells), F32),
            pltpu.VMEM((sx + TX, cells), F32),
            pltpu.VMEM((TX, cells), F32),
            dma((C, C.bit_length())),
            dma((C,)),
            dma((Q, R)),
            dma((Q, R)),
            dma((Q, R)),
            dma((Q, R)),
            dma((Q,)),
            dma((Q,)),
            dma((C,)),
            dma((C,)),
            dma((R,)),
            dma((R,)),
            dma,
            dma,
            dma,
            dma,
        ],
        compiler_params=pltpu.CompilerParams(
            collective_id=0, has_side_effects=True, vmem_limit_bytes=40 * 1024 * 1024
        ),
    )(hamiltonian, density, ham_pattern, den_pattern, tile_basis, offsets)


def solution(mesh):
    in_specs = (
        P("row", ("rep", "col")),
        P(("rep", "row"), "col"),
        P("row", ("rep", "col")),
        P(("rep", "row"), "col"),
        P(None, None, "col"),
        P(("row", "rep")),
    )
    out_specs = (P(("row", "rep"), "col"), P(("row", "rep"), "col"))
    body = functools.partial(shards, mesh.shape["row"], mesh.shape["col"])
    return jax.shard_map(body, mesh=mesh, in_specs=in_specs, out_specs=out_specs, check_vma=False)
```

```python
import functools
import math

import jax
import jax.numpy as jnp
from jax import lax
from jax.experimental import pallas as pl
from jax.experimental.pallas import tpu as pltpu
from jax.sharding import PartitionSpec as P

MESH = pl.DeviceIdType.MESH
TX = 16
LANES = 128
VMEM_MIB = 63
F32 = jnp.float32
BF16 = jnp.bfloat16
NT = (((1,), (1,)), ((), ()))


def flipped(index, mask):
    bit = 1
    while bit <= mask:
        if mask & bit:
            index = index + bit - 2 * bit * ((index // bit) % 2)
        bit *= 2
    return index


def low_bit(mask):
    return mask & -mask


def mask_row(pick, blocks, row, width):
    lane = lax.broadcasted_iota(jnp.int32, (1, width), 1) // (width // blocks)
    values = jnp.zeros((1, width), jnp.int32)
    for block in range(blocks):
        values = jnp.where(lane == block, pick(row, block), values)
    return values.astype(F32).astype(BF16)


def kernel(
    R, C, ham_in, den_in, hpat_in, dpat_in, basis_in, offsets_in, out, grid,
    ham, den, hpat, dpat, basis, offsets,
    hbuf, dbuf, psend, pown, precv, ssend, srecv, srow, tbuf, trecv, chcol, tiles, ext, incoming,
    hs, hr, drs, drr, dls, dlr, xs, xr, cs, cr, ws, wr, ts, tr, gs, gr, loaded, hello,
):
    r, c, p = lax.axis_index("row"), lax.axis_index("col"), lax.axis_index("rep")
    MR, KH = ham.shape
    KD, W = den.shape
    MH, Q, KHALF = MR // 2, W // LANES, C * KH
    atoms = offsets.shape[0]
    block = MH // atoms
    sx = grid.shape[0]
    slab, slabs = r * 2 + p, R * 2
    after, before = (slab + 1) % slabs, (slab + slabs - 1) % slabs
    next_id = {"row": after // 2, "rep": after % 2}
    last_id = {"row": before // 2, "rep": before % 2}
    peer = {"rep": 1 - p}

    bits = [1 << k for k in range(C.bit_length() - 1)]
    even = c % 2 == 0
    partner = {"col": flipped(c, 1)}

    barrier = pltpu.get_barrier_semaphore()
    friends = [{"row": (r + k) % R} for k in range(1, R)] + [{"col": flipped(c, bit)} for bit in bits[1:]]
    friends += [peer, next_id, last_id]
    for friend in friends:
        pl.semaphore_signal(barrier, inc=1, device_id=friend, device_id_type=MESH)

    @pl.when(even)
    def _():
        pl.semaphore_signal(barrier, inc=1, device_id=partner, device_id_type=MESH)

    pairs = [(dpat_in, dpat), (den_in, den), (hpat_in, hpat), (ham_in, ham), (basis_in, basis), (offsets_in, offsets)]
    loads = [pltpu.make_async_copy(a, b, loaded.at[k]) for k, (a, b) in enumerate(pairs)]
    for load in loads:
        load.start()

    def remote(src, dst, send, recv, to):
        return pltpu.make_async_remote_copy(
            src_ref=src, dst_ref=dst, send_sem=send, recv_sem=recv, device_id=to, device_id_type=MESH
        )

    def den_rows(q, owner):
        return dbuf.at[q, pl.ds(pl.multiple_of(owner * KD, KD), KD), :]

    def to_right(q, d):
        rows = den_rows(q, (r - d + R) % R)
        return remote(rows, rows, drs.at[q, d], drr.at[q, d + 1], {"row": (r + 1) % R})

    def to_left(q, d):
        rows = den_rows(q, (r + d) % R)
        return remote(rows, rows, dls.at[q, d], dlr.at[q, d + 1], {"row": (r + R - 1) % R})

    def send_right(q, d):
        @pl.when(jnp.logical_and(r - d >= 0, r + 1 < R))
        def _():
            to_right(q, d).start()

    def send_left(q, d):
        @pl.when(jnp.logical_and(r + d < R, r >= 1))
        def _():
            to_left(q, d).start()

    def own(q):
        send_right(q, 0)
        send_left(q, 0)

    def arrive(q, d):
        @pl.when(r - d >= 0)
        def _():
            rows = den_rows(q, (r - d + R) % R)
            remote(rows, rows, drs.at[q, d], drr.at[q, d], {"row": (r + 1) % R}).wait_recv()

        if d < R - 1:
            send_right(q, d)

        @pl.when(r + d < R)
        def _():
            rows = den_rows(q, (r + d) % R)
            remote(rows, rows, dls.at[q, d], dlr.at[q, d], {"row": (r + R - 1) % R}).wait_recv()

        if d < R - 1:
            send_left(q, d)

    def ham_copy(mask, bit):
        source = hbuf.at[flipped(c, mask)]
        return remote(source, source, hs.at[mask, bit.bit_length() - 1], hr.at[mask | bit], {"col": flipped(c, bit)})

    def ham_forward(mask):
        for bit in reversed(bits):
            if bit < low_bit(mask):
                ham_copy(mask, bit).start()

    def ham_arrive():
        for mask in sorted(range(1, C), key=lambda m: (-low_bit(m), m)):
            source = hbuf.at[flipped(c, mask)]
            remote(source, source, hs.at[mask, 0], hr.at[mask], {"col": flipped(c, 1)}).wait_recv()
            ham_forward(mask)

    loads[0].wait()
    loads[1].wait()
    dmasks = [mask_row(lambda i, j: dpat[i, j], dpat.shape[1], a, W) for a in range(dpat.shape[0])]
    tall = KD // dpat.shape[0]

    def mask_den(q):
        for a, values in enumerate(dmasks):
            rows = pl.ds(pl.multiple_of(r * KD + a * tall, tall), tall)
            dbuf[q, rows, :] = den[a * tall : (a + 1) * tall, q * LANES : (q + 1) * LANES] * values[:, q * LANES : (q + 1) * LANES]

    def mask_ham():
        high = MR // hpat.shape[1]
        for a in range(hpat.shape[1]):
            hbuf[c, a * high : (a + 1) * high, :] = ham[a * high : (a + 1) * high, :] * mask_row(lambda i, j: hpat[j, i], hpat.shape[0], a, KH)

    mask_den(0)
    loads[2].wait()
    loads[3].wait()
    mask_ham()

    @pl.when(even)
    def _():
        pl.semaphore_wait(barrier, len(friends))

    @pl.when(jnp.logical_not(even))
    def _():
        pl.semaphore_wait(barrier, len(friends) + 1)

    own(0)
    for bit in bits[1:]:
        ham_copy(0, bit).start()

    @pl.when(jnp.logical_not(even))
    def _():
        pl.semaphore_signal(hello, inc=1, device_id=partner, device_id_type=MESH)

    for q in range(1, Q):
        mask_den(q)
        if q == 1:
            own(1)

    ones = jnp.ones((16, LANES), BF16)
    mine = jnp.zeros((16, KD), F32)
    for q in range(Q):
        mine += lax.dot_general(ones, den_rows(q, r)[...], NT, preferred_element_type=F32)
    ssend[len(bits) - 1] = mine[:8]

    def s_copy(k):
        return remote(ssend.at[k], srecv.at[k], cs.at[k], cr.at[k], {"col": flipped(c, bits[k])})

    for load in loads[4:]:
        load.wait()
    if len(bits) > 1:
        s_copy(len(bits) - 1).start()

    def row_copy(k):
        return remote(srow.at[r], srow.at[r], ws.at[k], wr.at[k], {"row": (r + k) % R})

    def sums_over_chips():
        for k in range(len(bits) - 1, 0, -1):
            s_copy(k).wait_recv()
            ssend[k - 1] = ssend[k] + srecv[k]
            if k > 1:
                s_copy(k - 1).start()

    def meet_partner():
        @pl.when(even)
        def _():
            pl.semaphore_wait(hello, 1)

        ham_copy(0, 1).start()
        s_copy(0).start()

    def sums_over_cores():
        s_copy(0).wait_recv()
        srow[r] = ssend[0] + srecv[0]
        for k in range(1, R):
            row_copy(k).start()

    def t_copy():
        return remote(tbuf.at[1 - p], trecv, ts, tr, peer)

    def row_sums():
        for k in range(1, R):
            source = srow.at[(r - k + R) % R]
            remote(source, source, ws.at[k], wr.at[k], {"row": (r + k) % R}).wait_recv()
        step = min(KD, KH)
        total = jnp.zeros((24, MR), F32)
        for k in range(0, KHALF, step):
            piece = srow[k // KD, :, k % KD : k % KD + step]
            high_part = piece.astype(BF16).astype(F32)
            rest = piece - high_part
            mid_part = rest.astype(BF16).astype(F32)
            parts = jnp.concatenate([high_part, mid_part, rest - mid_part], axis=0).astype(BF16)
            total += lax.dot_general(
                parts, hbuf[k // KH, :, k % KH : k % KH + step], NT, preferred_element_type=F32
            )
        total = total[:8] + total[8:16] + total[16:]
        tbuf[0] = total[:, :MH]
        tbuf[1] = total[:, MH:]
        t_copy().start()

    def g_copy():
        return remote(ext.at[pl.ds(sx, TX), :], incoming, gs, gr, next_id)

    def collocate():
        t_copy().wait_recv()
        charges = (tbuf[p, 0:1, :] + trecv[0:1, :]) * (1.0 / math.sqrt(KHALF * 2))
        chcol[...] = jnp.transpose(jnp.broadcast_to(charges, (LANES, MH)))

        def body(m, sums):
            values = basis[m].astype(F32)
            return tuple(s + values * chcol[pl.ds(a * block + m, 1), :] for a, s in enumerate(sums))

        zero = jnp.zeros((TX, grid.shape[1]), F32)
        sums = lax.fori_loop(0, block, body, (zero,) * atoms, unroll=4)
        for a in range(atoms):
            tiles[a * TX : (a + 1) * TX, :] = sums[a]
        place = lax.broadcasted_iota(jnp.int32, (1, atoms * TX), 1)
        first = jnp.zeros((1, atoms * TX), jnp.int32)
        for a in range(atoms):
            first = jnp.where(place // TX == a, offsets[a], first)
        plane = lax.broadcasted_iota(jnp.int32, (sx + TX, atoms * TX), 0)
        onehot = jnp.where(plane == first + place % TX, 1.0, 0.0).astype(F32)
        ext[...] = jnp.dot(onehot, tiles[...], precision=lax.Precision.HIGHEST, preferred_element_type=F32)
        g_copy().start()

    def finish_grid():
        g_copy().wait_recv()
        grid[...] = ext[:sx, :]
        grid[:TX, :] = ext[:TX, :] + incoming[...]

    def x_copy(q):
        return remote(psend.at[q], precv.at[q], xs.at[q], xr.at[q], peer)

    def half(q, which):
        rows = pl.ds(pl.multiple_of(which * MH, MH), MH)
        total = jnp.zeros((MH, LANES), F32)
        for j in range(C):
            total += jnp.dot(hbuf[j, rows, :], dbuf[q, j * KH : (j + 1) * KH, :], preferred_element_type=F32)
        return total

    def multiply(q):
        psend[q] = half(q, 1 - p)
        x_copy(q).start()
        pown[q] = half(q, p)

    def drain(q):
        x_copy(q).wait_recv()
        out[:, q * LANES : (q + 1) * LANES] = (pown[q] + precv[q]).astype(BF16)

    hooks = {
        (0, 1): [sums_over_chips],
        (0, R - 1): [meet_partner, ham_arrive, sums_over_cores],
        (1, 1): [row_sums, lambda: multiply(0)],
        (1, R - 1): [lambda: multiply(1)],
        (2, 1): [collocate],
        (2, R - 1): [lambda: multiply(2), lambda: drain(0)],
        (3, 1): [finish_grid, lambda: drain(1)],
        (3, R - 1): [lambda: multiply(3), lambda: drain(2), lambda: drain(3)],
    }
    for q in range(Q):
        for d in range(1, R):
            arrive(q, d)
            if d == R - 1 and q + 2 < Q:
                own(q + 2)
            for hook in hooks.get((q, d), []):
                hook()

    for q in range(Q):
        x_copy(q).wait_send()
        for d in range(R - 1):
            @pl.when(jnp.logical_and(r - d >= 0, r + 1 < R))
            def _():
                to_right(q, d).wait_send()

            @pl.when(jnp.logical_and(r + d < R, r >= 1))
            def _():
                to_left(q, d).wait_send()

    for mask in range(C):
        for bit in bits:
            if mask == 0 or bit < low_bit(mask):
                ham_copy(mask, bit).wait_send()
    for k in range(len(bits)):
        s_copy(k).wait_send()
    for k in range(1, R):
        row_copy(k).wait_send()
    t_copy().wait_send()
    g_copy().wait_send()


def shards(R, C, hamiltonian, density, ham_pattern, den_pattern, tile_basis, offsets):
    MR, KH = hamiltonian.shape
    KD, W = density.shape
    MH, Q, KHALF = MR // 2, W // LANES, C * KH
    cells, atoms = tile_basis.shape[2], offsets.shape[0]
    sx = 32
    dma = pltpu.SemaphoreType.DMA
    vmem = pl.BlockSpec(memory_space=pltpu.VMEM)
    hbm = pl.BlockSpec(memory_space=pltpu.HBM)
    return pl.pallas_call(
        functools.partial(kernel, R, C),
        out_shape=(jax.ShapeDtypeStruct((MH, W), BF16), jax.ShapeDtypeStruct((sx, cells), F32)),
        in_specs=[hbm] * 6,
        out_specs=(vmem, vmem),
        scratch_shapes=[
            pltpu.VMEM((MR, KH), BF16),
            pltpu.VMEM((KD, W), BF16),
            pltpu.SMEM(ham_pattern.shape[::-1], jnp.int32),
            pltpu.SMEM(den_pattern.shape, jnp.int32),
            pltpu.VMEM(tile_basis.shape, BF16),
            pltpu.SMEM(offsets.shape, jnp.int32),
            pltpu.VMEM((C, MR, KH), BF16),
            pltpu.VMEM((Q, KHALF, LANES), BF16),
            pltpu.VMEM((Q, MH, LANES), F32),
            pltpu.VMEM((Q, MH, LANES), F32),
            pltpu.VMEM((Q, MH, LANES), F32),
            pltpu.VMEM((C.bit_length(), 8, KD), F32),
            pltpu.VMEM((C.bit_length(), 8, KD), F32),
            pltpu.VMEM((R, 8, KD), F32),
            pltpu.VMEM((2, 8, MH), F32),
            pltpu.VMEM((8, MH), F32),
            pltpu.VMEM((MH, LANES), F32),
            pltpu.VMEM((atoms * TX, cells), F32),
            pltpu.VMEM((sx + TX, cells), F32),
            pltpu.VMEM((TX, cells), F32),
            dma((C, C.bit_length())),
            dma((C,)),
            dma((Q, R)),
            dma((Q, R)),
            dma((Q, R)),
            dma((Q, R)),
            dma((Q,)),
            dma((Q,)),
            dma((C.bit_length(),)),
            dma((C.bit_length(),)),
            dma((R,)),
            dma((R,)),
            dma,
            dma,
            dma,
            dma,
            dma((6,)),
            pltpu.SemaphoreType.REGULAR,
        ],
        compiler_params=pltpu.CompilerParams(
            collective_id=0, has_side_effects=True, vmem_limit_bytes=VMEM_MIB * 1024 * 1024
        ),
    )(hamiltonian, density, ham_pattern.T, den_pattern, tile_basis, offsets)


def solution(mesh):
    in_specs = (
        P("row", ("rep", "col")),
        P(("rep", "row"), "col"),
        P("row", ("rep", "col")),
        P(("rep", "row"), "col"),
        P(None, None, "col"),
        P(("row", "rep")),
    )
    out_specs = (P(("row", "rep"), "col"), P(("row", "rep"), "col"))
    body = functools.partial(shards, mesh.shape["row"], mesh.shape["col"])
    return jax.shard_map(body, mesh=mesh, in_specs=in_specs, out_specs=out_specs, check_vma=False)
```

```python
import functools
import math

import jax
import jax.numpy as jnp
from jax import lax
from jax.experimental import pallas as pl
from jax.experimental.pallas import tpu as pltpu
from jax.sharding import PartitionSpec as P

MESH = pl.DeviceIdType.MESH
TX = 16
LANES = 128
VMEM_MIB = 63
F32 = jnp.float32
BF16 = jnp.bfloat16
NT = (((1,), (1,)), ((), ()))


def flipped(index, mask):
    bit = 1
    while bit <= mask:
        if mask & bit:
            index = index + bit - 2 * bit * ((index // bit) % 2)
        bit *= 2
    return index


def low_bit(mask):
    return mask & -mask


def mask_row(pick, blocks, row, width):
    lane = lax.broadcasted_iota(jnp.int32, (1, width), 1) // (width // blocks)
    values = jnp.zeros((1, width), jnp.int32)
    for block in range(blocks):
        values = jnp.where(lane == block, pick(row, block), values)
    return values.astype(F32).astype(BF16)


def kernel(
    R, C, ham_in, den_in, hpat_in, dpat_in, basis_in, offsets_in, out, grid,
    ham, den, hpat, dpat, basis, offsets,
    hbuf, dbuf, psend, pown, precv, ssend, srecv, srow, tbuf, trecv, chcol, tiles, ext, incoming, done, stored,
    hs, hr, drs, drr, dls, dlr, xs, xr, cs, cr, ws, wr, ts, tr, gs, gr, loaded, hello,
):
    r, c, p = lax.axis_index("row"), lax.axis_index("col"), lax.axis_index("rep")
    MR, KH = ham.shape
    KD, W = den.shape
    MH, Q, KHALF = MR // 2, W // LANES, C * KH
    atoms = offsets.shape[0]
    block = MH // atoms
    sx = grid.shape[0]
    slab, slabs = r * 2 + p, R * 2
    after, before = (slab + 1) % slabs, (slab + slabs - 1) % slabs
    next_id = {"row": after // 2, "rep": after % 2}
    last_id = {"row": before // 2, "rep": before % 2}
    peer = {"rep": 1 - p}

    bits = [1 << k for k in range(C.bit_length() - 1)]
    even = c % 2 == 0
    partner = {"col": flipped(c, 1)}

    barrier = pltpu.get_barrier_semaphore()
    friends = [{"row": (r + k) % R} for k in range(1, R)] + [{"col": flipped(c, bit)} for bit in bits[1:]]
    friends += [peer, next_id, last_id]
    for friend in friends:
        pl.semaphore_signal(barrier, inc=1, device_id=friend, device_id_type=MESH)

    @pl.when(even)
    def _():
        pl.semaphore_signal(barrier, inc=1, device_id=partner, device_id_type=MESH)

    pairs = [(dpat_in, dpat), (den_in, den), (hpat_in, hpat), (ham_in, ham), (basis_in, basis), (offsets_in, offsets)]
    loads = [pltpu.make_async_copy(a, b, loaded.at[k]) for k, (a, b) in enumerate(pairs)]
    for load in loads:
        load.start()

    def remote(src, dst, send, recv, to):
        return pltpu.make_async_remote_copy(
            src_ref=src, dst_ref=dst, send_sem=send, recv_sem=recv, device_id=to, device_id_type=MESH
        )

    def den_rows(q, owner):
        return dbuf.at[q, pl.ds(pl.multiple_of(owner * KD, KD), KD), :]

    def to_right(q, d):
        rows = den_rows(q, (r - d + R) % R)
        return remote(rows, rows, drs.at[q, d], drr.at[q, d + 1], {"row": (r + 1) % R})

    def to_left(q, d):
        rows = den_rows(q, (r + d) % R)
        return remote(rows, rows, dls.at[q, d], dlr.at[q, d + 1], {"row": (r + R - 1) % R})

    def send_right(q, d):
        @pl.when(jnp.logical_and(r - d >= 0, r + 1 < R))
        def _():
            to_right(q, d).start()

    def send_left(q, d):
        @pl.when(jnp.logical_and(r + d < R, r >= 1))
        def _():
            to_left(q, d).start()

    def own(q):
        send_right(q, 0)
        send_left(q, 0)

    def arrive(q, d):
        @pl.when(r - d >= 0)
        def _():
            rows = den_rows(q, (r - d + R) % R)
            remote(rows, rows, drs.at[q, d], drr.at[q, d], {"row": (r + 1) % R}).wait_recv()

        if d < R - 1:
            send_right(q, d)

        @pl.when(r + d < R)
        def _():
            rows = den_rows(q, (r + d) % R)
            remote(rows, rows, dls.at[q, d], dlr.at[q, d], {"row": (r + R - 1) % R}).wait_recv()

        if d < R - 1:
            send_left(q, d)

    def ham_copy(mask, bit):
        source = hbuf.at[flipped(c, mask)]
        return remote(source, source, hs.at[mask, bit.bit_length() - 1], hr.at[mask | bit], {"col": flipped(c, bit)})

    def ham_forward(mask):
        for bit in reversed(bits):
            if bit < low_bit(mask):
                ham_copy(mask, bit).start()

    def ham_arrive():
        for mask in sorted(range(1, C), key=lambda m: (-low_bit(m), m)):
            source = hbuf.at[flipped(c, mask)]
            remote(source, source, hs.at[mask, 0], hr.at[mask], {"col": flipped(c, 1)}).wait_recv()
            ham_forward(mask)

    loads[0].wait()
    loads[1].wait()
    dmasks = [mask_row(lambda i, j: dpat[i, j], dpat.shape[1], a, W) for a in range(dpat.shape[0])]
    tall = KD // dpat.shape[0]

    def mask_den(q):
        for a, values in enumerate(dmasks):
            rows = pl.ds(pl.multiple_of(r * KD + a * tall, tall), tall)
            dbuf[q, rows, :] = den[a * tall : (a + 1) * tall, q * LANES : (q + 1) * LANES] * values[:, q * LANES : (q + 1) * LANES]

    def mask_ham():
        high = MR // hpat.shape[1]
        for a in range(hpat.shape[1]):
            hbuf[c, a * high : (a + 1) * high, :] = ham[a * high : (a + 1) * high, :] * mask_row(lambda i, j: hpat[j, i], hpat.shape[0], a, KH)

    for q in range(Q):
        mask_den(q)

    ones = jnp.ones((16, LANES), BF16)
    mine = jnp.zeros((16, KD), F32)
    for q in range(Q):
        mine += lax.dot_general(ones, den_rows(q, r)[...], NT, preferred_element_type=F32)
    ssend[len(bits) - 1] = mine[:8]

    def s_copy(k):
        return remote(ssend.at[k], srecv.at[k], cs.at[k], cr.at[k], {"col": flipped(c, bits[k])})

    loads[2].wait()
    loads[3].wait()
    mask_ham()

    @pl.when(even)
    def _():
        pl.semaphore_wait(barrier, len(friends))

    @pl.when(jnp.logical_not(even))
    def _():
        pl.semaphore_wait(barrier, len(friends) + 1)

    if len(bits) > 1:
        s_copy(len(bits) - 1).start()
    for q in range(min(3, Q)):
        own(q)
    for bit in bits[1:]:
        ham_copy(0, bit).start()

    @pl.when(jnp.logical_not(even))
    def _():
        pl.semaphore_signal(hello, inc=1, device_id=partner, device_id_type=MESH)

    for load in loads[4:]:
        load.wait()

    def row_copy(k):
        return remote(srow.at[r], srow.at[r], ws.at[k], wr.at[k], {"row": (r + k) % R})

    def sums_over_chips():
        for k in range(len(bits) - 1, 0, -1):
            s_copy(k).wait_recv()
            ssend[k - 1] = ssend[k] + srecv[k]
            if k > 1:
                s_copy(k - 1).start()

    def meet_partner():
        @pl.when(even)
        def _():
            pl.semaphore_wait(hello, 1)

        ham_copy(0, 1).start()
        s_copy(0).start()

    def sums_over_cores():
        s_copy(0).wait_recv()
        srow[r] = ssend[0] + srecv[0]
        for k in range(1, R):
            row_copy(k).start()

    def t_copy():
        return remote(tbuf.at[1 - p], trecv, ts, tr, peer)

    def row_sums():
        for k in range(1, R):
            source = srow.at[(r - k + R) % R]
            remote(source, source, ws.at[k], wr.at[k], {"row": (r + k) % R}).wait_recv()
        step = min(KD, KH)
        total = jnp.zeros((24, MR), F32)
        for k in range(0, KHALF, step):
            piece = srow[k // KD, :, k % KD : k % KD + step]
            high_part = piece.astype(BF16).astype(F32)
            rest = piece - high_part
            mid_part = rest.astype(BF16).astype(F32)
            parts = jnp.concatenate([high_part, mid_part, rest - mid_part], axis=0).astype(BF16)
            total += lax.dot_general(
                parts, hbuf[k // KH, :, k % KH : k % KH + step], NT, preferred_element_type=F32
            )
        total = total[:8] + total[8:16] + total[16:]
        tbuf[0] = total[:, :MH]
        tbuf[1] = total[:, MH:]
        t_copy().start()

    def g_copy():
        return remote(ext.at[pl.ds(sx, TX), :], incoming, gs, gr, next_id)

    def collocate():
        t_copy().wait_recv()
        charges = (tbuf[p, 0:1, :] + trecv[0:1, :]) * (1.0 / math.sqrt(KHALF * 2))
        chcol[...] = jnp.transpose(jnp.broadcast_to(charges, (LANES, MH)))

        def body(m, sums):
            values = basis[m].astype(F32)
            return tuple(s + values * chcol[pl.ds(a * block + m, 1), :] for a, s in enumerate(sums))

        zero = jnp.zeros((TX, grid.shape[1]), F32)
        sums = lax.fori_loop(0, block, body, (zero,) * atoms, unroll=4)
        for a in range(atoms):
            tiles[a * TX : (a + 1) * TX, :] = sums[a]
        place = lax.broadcasted_iota(jnp.int32, (1, atoms * TX), 1)
        first = jnp.zeros((1, atoms * TX), jnp.int32)
        for a in range(atoms):
            first = jnp.where(place // TX == a, offsets[a], first)
        plane = lax.broadcasted_iota(jnp.int32, (sx + TX, atoms * TX), 0)
        onehot = jnp.where(plane == first + place % TX, 1.0, 0.0).astype(F32)
        ext[...] = jnp.dot(onehot, tiles[...], precision=lax.Precision.HIGHEST, preferred_element_type=F32)
        g_copy().start()

    def finish_grid():
        g_copy().wait_recv()
        ext[:TX, :] = ext[:TX, :] + incoming[...]
        grid_copy().start()

    def x_copy(q):
        return remote(psend.at[q], precv.at[q], xs.at[q], xr.at[q], peer)

    def half(q, which):
        rows = pl.ds(pl.multiple_of(which * MH, MH), MH)
        total = jnp.zeros((MH, LANES), F32)
        for j in range(C):
            total += jnp.dot(hbuf[j, rows, :], dbuf[q, j * KH : (j + 1) * KH, :], preferred_element_type=F32)
        return total

    def multiply(q):
        psend[q] = half(q, 1 - p)
        x_copy(q).start()
        pown[q] = half(q, p)

    def out_copy(q):
        return pltpu.make_async_copy(done.at[q], out.at[:, pl.ds(q * LANES, LANES)], stored.at[q])

    def grid_copy():
        return pltpu.make_async_copy(ext.at[pl.ds(0, sx), :], grid, stored.at[Q])

    def drain(q):
        x_copy(q).wait_recv()
        done[q] = (pown[q] + precv[q]).astype(BF16)
        out_copy(q).start()

    hooks = {
        (0, 1): [sums_over_chips, meet_partner],
        (1, 1): [sums_over_cores],
        (0, 2): [ham_arrive],
        (0, R - 1): [lambda: multiply(0)],
        (2, 1): [row_sums],
        (1, R - 1): [lambda: multiply(1), collocate],
        (2, R - 1): [lambda: multiply(2), lambda: drain(0), finish_grid],
        (3, R - 2): [lambda: drain(1)],
        (3, R - 1): [lambda: multiply(3), lambda: drain(2), lambda: drain(3)],
    }
    steps = [(q, d) for q in range(Q) for d in range(1, R)]
    for q, d in sorted(steps, key=lambda step: (step[0] + (step[1] > 1), step[1] > 1, step[1])):
        arrive(q, d)
        if d == 1 and q >= 1 and q + 2 < Q:
            own(q + 2)
        for hook in hooks.get((q, d), []):
            hook()

    for q in range(Q):
        x_copy(q).wait_send()
        for d in range(R - 1):
            @pl.when(jnp.logical_and(r - d >= 0, r + 1 < R))
            def _():
                to_right(q, d).wait_send()

            @pl.when(jnp.logical_and(r + d < R, r >= 1))
            def _():
                to_left(q, d).wait_send()

    for mask in range(C):
        for bit in bits:
            if mask == 0 or bit < low_bit(mask):
                ham_copy(mask, bit).wait_send()
    for k in range(len(bits)):
        s_copy(k).wait_send()
    for k in range(1, R):
        row_copy(k).wait_send()
    t_copy().wait_send()
    g_copy().wait_send()
    for q in range(Q):
        out_copy(q).wait()
    grid_copy().wait()


def hand_on(product, planes, out, grid, sems):
    copies = [pltpu.make_async_copy(product, out, sems.at[0]), pltpu.make_async_copy(planes, grid, sems.at[1])]
    for copy in copies:
        copy.start()
    for copy in copies:
        copy.wait()


def shards(R, C, hamiltonian, density, ham_pattern, den_pattern, tile_basis, offsets):
    MR, KH = hamiltonian.shape
    KD, W = density.shape
    MH, Q, KHALF = MR // 2, W // LANES, C * KH
    cells, atoms = tile_basis.shape[2], offsets.shape[0]
    sx = 32
    dma = pltpu.SemaphoreType.DMA
    hbm = pl.BlockSpec(memory_space=pltpu.HBM)
    results = pl.pallas_call(
        functools.partial(kernel, R, C),
        out_shape=(jax.ShapeDtypeStruct((MH, W), BF16), jax.ShapeDtypeStruct((sx, cells), F32)),
        in_specs=[hbm] * 6,
        out_specs=(hbm, hbm),
        scratch_shapes=[
            pltpu.VMEM((MR, KH), BF16),
            pltpu.VMEM((KD, W), BF16),
            pltpu.SMEM(ham_pattern.shape[::-1], jnp.int32),
            pltpu.SMEM(den_pattern.shape, jnp.int32),
            pltpu.VMEM(tile_basis.shape, BF16),
            pltpu.SMEM(offsets.shape, jnp.int32),
            pltpu.VMEM((C, MR, KH), BF16),
            pltpu.VMEM((Q, KHALF, LANES), BF16),
            pltpu.VMEM((Q, MH, LANES), F32),
            pltpu.VMEM((Q, MH, LANES), F32),
            pltpu.VMEM((Q, MH, LANES), F32),
            pltpu.VMEM((C.bit_length(), 8, KD), F32),
            pltpu.VMEM((C.bit_length(), 8, KD), F32),
            pltpu.VMEM((R, 8, KD), F32),
            pltpu.VMEM((2, 8, MH), F32),
            pltpu.VMEM((8, MH), F32),
            pltpu.VMEM((MH, LANES), F32),
            pltpu.VMEM((atoms * TX, cells), F32),
            pltpu.VMEM((sx + TX, cells), F32),
            pltpu.VMEM((TX, cells), F32),
            pltpu.VMEM((Q, MH, LANES), BF16),
            dma((Q + 1,)),
            dma((C, C.bit_length())),
            dma((C,)),
            dma((Q, R)),
            dma((Q, R)),
            dma((Q, R)),
            dma((Q, R)),
            dma((Q,)),
            dma((Q,)),
            dma((C.bit_length(),)),
            dma((C.bit_length(),)),
            dma((R,)),
            dma((R,)),
            dma,
            dma,
            dma,
            dma,
            dma((6,)),
            pltpu.SemaphoreType.REGULAR,
        ],
        compiler_params=pltpu.CompilerParams(
            collective_id=0, has_side_effects=True, vmem_limit_bytes=VMEM_MIB * 1024 * 1024
        ),
    )(hamiltonian, density, ham_pattern.T, den_pattern, tile_basis, offsets)
    return pl.pallas_call(
        hand_on,
        out_shape=tuple(jax.ShapeDtypeStruct(x.shape, x.dtype) for x in results),
        in_specs=[hbm, hbm],
        out_specs=(hbm, hbm),
        scratch_shapes=[dma((2,))],
        compiler_params=pltpu.CompilerParams(vmem_limit_bytes=VMEM_MIB * 1024 * 1024),
    )(*results)


def solution(mesh):
    in_specs = (
        P("row", ("rep", "col")),
        P(("rep", "row"), "col"),
        P("row", ("rep", "col")),
        P(("rep", "row"), "col"),
        P(None, None, "col"),
        P(("row", "rep")),
    )
    out_specs = (P(("row", "rep"), "col"), P(("row", "rep"), "col"))
    body = functools.partial(shards, mesh.shape["row"], mesh.shape["col"])
    return jax.shard_map(body, mesh=mesh, in_specs=in_specs, out_specs=out_specs, check_vma=False)
```

```python
import functools
import math

import jax
import jax.numpy as jnp
from jax import lax
from jax.experimental import pallas as pl
from jax.experimental.pallas import tpu as pltpu
from jax.sharding import PartitionSpec as P

MESH = pl.DeviceIdType.MESH
TX = 16
LANES = 128
VMEM_KIB = 65536 - 512
F32 = jnp.float32
BF16 = jnp.bfloat16
NT = (((1,), (1,)), ((), ()))


def flipped(index, mask):
    bit = 1
    while bit <= mask:
        if mask & bit:
            index = index + bit - 2 * bit * ((index // bit) % 2)
        bit *= 2
    return index


def low_bit(mask):
    return mask & -mask


def mask_row(pick, blocks, row, width):
    lane = lax.broadcasted_iota(jnp.int32, (1, width), 1) // (width // blocks)
    values = jnp.zeros((1, width), jnp.int32)
    for block in range(blocks):
        values = jnp.where(lane == block, pick(row, block), values)
    return values.astype(F32).astype(BF16)


def kernel(
    R, C, ham_in, den_in, hpat_in, dpat_in, basis_in, offsets_in, out, grid,
    ham, den, hpat, dpat, basis, offsets,
    hbuf, dbuf, psend, pown, precv, ssend, srecv, srow, tbuf, trecv, chcol, tiles, ext, incoming,
    hs, hr, drs, drr, dls, dlr, xs, xr, cs, cr, ws, wr, ts, tr, gs, gr, loaded, hello,
):
    r, c, p = lax.axis_index("row"), lax.axis_index("col"), lax.axis_index("rep")
    MR, KH = ham.shape
    KD, W = den.shape
    MH, Q, KHALF = MR // 2, W // LANES, C * KH
    atoms = offsets.shape[0]
    block = MH // atoms
    sx = grid.shape[0]
    slab, slabs = r * 2 + p, R * 2
    after, before = (slab + 1) % slabs, (slab + slabs - 1) % slabs
    next_id = {"row": after // 2, "rep": after % 2}
    last_id = {"row": before // 2, "rep": before % 2}
    peer = {"rep": 1 - p}

    bits = [1 << k for k in range(C.bit_length() - 1)]
    even = c % 2 == 0
    partner = {"col": flipped(c, 1)}

    barrier = pltpu.get_barrier_semaphore()
    friends = [{"row": (r + k) % R} for k in range(1, R)] + [{"col": flipped(c, bit)} for bit in bits[1:]]
    friends += [peer, next_id, last_id]
    for friend in friends:
        pl.semaphore_signal(barrier, inc=1, device_id=friend, device_id_type=MESH)

    @pl.when(even)
    def _():
        pl.semaphore_signal(barrier, inc=1, device_id=partner, device_id_type=MESH)

    pairs = [(dpat_in, dpat), (den_in, den), (hpat_in, hpat), (ham_in, ham), (basis_in, basis), (offsets_in, offsets)]
    loads = [pltpu.make_async_copy(a, b, loaded.at[k]) for k, (a, b) in enumerate(pairs)]
    for load in loads:
        load.start()

    def remote(src, dst, send, recv, to):
        return pltpu.make_async_remote_copy(
            src_ref=src, dst_ref=dst, send_sem=send, recv_sem=recv, device_id=to, device_id_type=MESH
        )

    def den_rows(q, owner):
        return dbuf.at[q, pl.ds(pl.multiple_of(owner * KD, KD), KD), :]

    def to_right(q, d):
        rows = den_rows(q, (r - d + R) % R)
        return remote(rows, rows, drs.at[q, d], drr.at[q, d + 1], {"row": (r + 1) % R})

    def to_left(q, d):
        rows = den_rows(q, (r + d) % R)
        return remote(rows, rows, dls.at[q, d], dlr.at[q, d + 1], {"row": (r + R - 1) % R})

    def send_right(q, d):
        @pl.when(jnp.logical_and(r - d >= 0, r + 1 < R))
        def _():
            to_right(q, d).start()

    def send_left(q, d):
        @pl.when(jnp.logical_and(r + d < R, r >= 1))
        def _():
            to_left(q, d).start()

    def own(q):
        send_right(q, 0)
        send_left(q, 0)

    def arrive(q, d):
        @pl.when(r - d >= 0)
        def _():
            rows = den_rows(q, (r - d + R) % R)
            remote(rows, rows, drs.at[q, d], drr.at[q, d], {"row": (r + 1) % R}).wait_recv()

        if d < R - 1:
            send_right(q, d)

        @pl.when(r + d < R)
        def _():
            rows = den_rows(q, (r + d) % R)
            remote(rows, rows, dls.at[q, d], dlr.at[q, d], {"row": (r + R - 1) % R}).wait_recv()

        if d < R - 1:
            send_left(q, d)

    def ham_copy(mask, bit):
        source = hbuf.at[flipped(c, mask)]
        return remote(source, source, hs.at[mask, bit.bit_length() - 1], hr.at[mask | bit], {"col": flipped(c, bit)})

    def ham_forward(mask):
        for bit in reversed(bits):
            if bit < low_bit(mask):
                ham_copy(mask, bit).start()

    def ham_arrive():
        for mask in sorted(range(1, C), key=lambda m: (-low_bit(m), m)):
            source = hbuf.at[flipped(c, mask)]
            remote(source, source, hs.at[mask, 0], hr.at[mask], {"col": flipped(c, 1)}).wait_recv()
            ham_forward(mask)

    loads[0].wait()
    loads[1].wait()
    dmasks = [mask_row(lambda i, j: dpat[i, j], dpat.shape[1], a, W) for a in range(dpat.shape[0])]
    tall = KD // dpat.shape[0]

    def mask_den(q):
        for a, values in enumerate(dmasks):
            rows = pl.ds(pl.multiple_of(r * KD + a * tall, tall), tall)
            dbuf[q, rows, :] = den[a * tall : (a + 1) * tall, q * LANES : (q + 1) * LANES] * values[:, q * LANES : (q + 1) * LANES]

    def mask_ham():
        high = MR // hpat.shape[1]
        for a in range(hpat.shape[1]):
            hbuf[c, a * high : (a + 1) * high, :] = ham[a * high : (a + 1) * high, :] * mask_row(lambda i, j: hpat[j, i], hpat.shape[0], a, KH)

    for q in range(Q):
        mask_den(q)

    ones = jnp.ones((16, LANES), BF16)
    mine = jnp.zeros((16, KD), F32)
    for q in range(Q):
        mine += lax.dot_general(ones, den_rows(q, r)[...], NT, preferred_element_type=F32)
    ssend[len(bits) - 1] = mine[:8]

    def s_copy(k):
        return remote(ssend.at[k], srecv.at[k], cs.at[k], cr.at[k], {"col": flipped(c, bits[k])})

    loads[2].wait()
    loads[3].wait()
    mask_ham()

    @pl.when(even)
    def _():
        pl.semaphore_wait(barrier, len(friends))

    @pl.when(jnp.logical_not(even))
    def _():
        pl.semaphore_wait(barrier, len(friends) + 1)

    if len(bits) > 1:
        s_copy(len(bits) - 1).start()
    for q in range(min(3, Q)):
        own(q)
    for bit in bits[1:]:
        ham_copy(0, bit).start()

    @pl.when(jnp.logical_not(even))
    def _():
        pl.semaphore_signal(hello, inc=1, device_id=partner, device_id_type=MESH)

    for load in loads[4:]:
        load.wait()

    def row_copy(k):
        return remote(srow.at[r], srow.at[r], ws.at[k], wr.at[k], {"row": (r + k) % R})

    def sums_over_chips():
        for k in range(len(bits) - 1, 0, -1):
            s_copy(k).wait_recv()
            ssend[k - 1] = ssend[k] + srecv[k]
            if k > 1:
                s_copy(k - 1).start()

    def meet_partner():
        @pl.when(even)
        def _():
            pl.semaphore_wait(hello, 1)

        ham_copy(0, 1).start()
        s_copy(0).start()

    def sums_over_cores():
        s_copy(0).wait_recv()
        srow[r] = ssend[0] + srecv[0]
        for k in range(1, R):
            row_copy(k).start()

    def t_copy():
        return remote(tbuf.at[1 - p], trecv, ts, tr, peer)

    def row_sums():
        for k in range(1, R):
            source = srow.at[(r - k + R) % R]
            remote(source, source, ws.at[k], wr.at[k], {"row": (r + k) % R}).wait_recv()
        step = min(KD, KH)
        total = jnp.zeros((24, MR), F32)
        for k in range(0, KHALF, step):
            piece = srow[k // KD, :, k % KD : k % KD + step]
            high_part = piece.astype(BF16).astype(F32)
            rest = piece - high_part
            mid_part = rest.astype(BF16).astype(F32)
            parts = jnp.concatenate([high_part, mid_part, rest - mid_part], axis=0).astype(BF16)
            total += lax.dot_general(
                parts, hbuf[k // KH, :, k % KH : k % KH + step], NT, preferred_element_type=F32
            )
        total = total[:8] + total[8:16] + total[16:]
        tbuf[0] = total[:, :MH]
        tbuf[1] = total[:, MH:]
        t_copy().start()

    def g_copy():
        return remote(ext.at[pl.ds(sx, TX), :], incoming, gs, gr, next_id)

    def collocate():
        t_copy().wait_recv()
        charges = (tbuf[p, 0:1, :] + trecv[0:1, :]) * (1.0 / math.sqrt(KHALF * 2))
        chcol[...] = jnp.transpose(jnp.broadcast_to(charges, (LANES, MH)))

        def body(m, sums):
            values = basis[m].astype(F32)
            return tuple(s + values * chcol[pl.ds(a * block + m, 1), :] for a, s in enumerate(sums))

        zero = jnp.zeros((TX, grid.shape[1]), F32)
        sums = lax.fori_loop(0, block, body, (zero,) * atoms, unroll=4)
        for a in range(atoms):
            tiles[a * TX : (a + 1) * TX, :] = sums[a]
        place = lax.broadcasted_iota(jnp.int32, (1, atoms * TX), 1)
        first = jnp.zeros((1, atoms * TX), jnp.int32)
        for a in range(atoms):
            first = jnp.where(place // TX == a, offsets[a], first)
        plane = lax.broadcasted_iota(jnp.int32, (sx + TX, atoms * TX), 0)
        onehot = jnp.where(plane == first + place % TX, 1.0, 0.0).astype(F32)
        ext[...] = jnp.dot(onehot, tiles[...], precision=lax.Precision.HIGHEST, preferred_element_type=F32)
        g_copy().start()

    def finish_grid():
        g_copy().wait_recv()
        grid[TX:, :] = ext[TX:sx, :]
        grid[:TX, :] = ext[:TX, :] + incoming[...]

    def x_copy(q):
        return remote(psend.at[q], precv.at[q], xs.at[q], xr.at[q], peer)

    def half(q, which):
        rows = pl.ds(pl.multiple_of(which * MH, MH), MH)
        total = jnp.zeros((MH, LANES), F32)
        for j in range(C):
            total += jnp.dot(hbuf[j, rows, :], dbuf[q, j * KH : (j + 1) * KH, :], preferred_element_type=F32)
        return total

    def multiply(q):
        psend[q] = half(q, 1 - p)
        x_copy(q).start()
        pown[q] = half(q, p)

    def drain(q):
        x_copy(q).wait_recv()
        out[:, q * LANES : (q + 1) * LANES] = (pown[q] + precv[q]).astype(BF16)

    hooks = {
        (0, 1): [sums_over_chips, meet_partner],
        (1, 1): [sums_over_cores],
        (0, 2): [ham_arrive],
        (0, R - 1): [lambda: multiply(0)],
        (2, 1): [row_sums],
        (1, R - 1): [lambda: multiply(1), collocate],
        (2, R - 1): [lambda: multiply(2), lambda: drain(0), finish_grid],
        (3, R - 2): [lambda: drain(1)],
        (3, R - 1): [lambda: multiply(3), lambda: drain(2), lambda: drain(3)],
    }
    steps = [(q, d) for q in range(Q) for d in range(1, R)]
    for q, d in sorted(steps, key=lambda step: (step[0] + (step[1] > 1), step[1] > 1, step[1])):
        arrive(q, d)
        if d == 1 and q >= 1 and q + 2 < Q:
            own(q + 2)
        for hook in hooks.get((q, d), []):
            hook()

    for q in range(Q):
        x_copy(q).wait_send()
        for d in range(R - 1):
            @pl.when(jnp.logical_and(r - d >= 0, r + 1 < R))
            def _():
                to_right(q, d).wait_send()

            @pl.when(jnp.logical_and(r + d < R, r >= 1))
            def _():
                to_left(q, d).wait_send()

    for mask in range(C):
        for bit in bits:
            if mask == 0 or bit < low_bit(mask):
                ham_copy(mask, bit).wait_send()
    for k in range(len(bits)):
        s_copy(k).wait_send()
    for k in range(1, R):
        row_copy(k).wait_send()
    t_copy().wait_send()
    g_copy().wait_send()


def shards(R, C, hamiltonian, density, ham_pattern, den_pattern, tile_basis, offsets):
    MR, KH = hamiltonian.shape
    KD, W = density.shape
    MH, Q, KHALF = MR // 2, W // LANES, C * KH
    cells, atoms = tile_basis.shape[2], offsets.shape[0]
    sx = 32
    dma = pltpu.SemaphoreType.DMA
    hbm = pl.BlockSpec(memory_space=pltpu.HBM)
    vmem = pl.BlockSpec(memory_space=pltpu.VMEM)
    return pl.pallas_call(
        functools.partial(kernel, R, C),
        out_shape=(jax.ShapeDtypeStruct((MH, W), BF16), jax.ShapeDtypeStruct((sx, cells), F32)),
        in_specs=[hbm] * 6,
        out_specs=(vmem, vmem),
        scratch_shapes=[
            pltpu.VMEM((MR, KH), BF16),
            pltpu.VMEM((KD, W), BF16),
            pltpu.SMEM(ham_pattern.shape[::-1], jnp.int32),
            pltpu.SMEM(den_pattern.shape, jnp.int32),
            pltpu.VMEM(tile_basis.shape, BF16),
            pltpu.SMEM(offsets.shape, jnp.int32),
            pltpu.VMEM((C, MR, KH), BF16),
            pltpu.VMEM((Q, KHALF, LANES), BF16),
            pltpu.VMEM((Q, MH, LANES), F32),
            pltpu.VMEM((Q, MH, LANES), F32),
            pltpu.VMEM((Q, MH, LANES), F32),
            pltpu.VMEM((C.bit_length(), 8, KD), F32),
            pltpu.VMEM((C.bit_length(), 8, KD), F32),
            pltpu.VMEM((R, 8, KD), F32),
            pltpu.VMEM((2, 8, MH), F32),
            pltpu.VMEM((8, MH), F32),
            pltpu.VMEM((MH, LANES), F32),
            pltpu.VMEM((atoms * TX, cells), F32),
            pltpu.VMEM((sx + TX, cells), F32),
            pltpu.VMEM((TX, cells), F32),
            dma((C, C.bit_length())),
            dma((C,)),
            dma((Q, R)),
            dma((Q, R)),
            dma((Q, R)),
            dma((Q, R)),
            dma((Q,)),
            dma((Q,)),
            dma((C.bit_length(),)),
            dma((C.bit_length(),)),
            dma((R,)),
            dma((R,)),
            dma,
            dma,
            dma,
            dma,
            dma((6,)),
            pltpu.SemaphoreType.REGULAR,
        ],
        compiler_params=pltpu.CompilerParams(
            collective_id=0, has_side_effects=True, vmem_limit_bytes=VMEM_KIB * 1024
        ),
    )(hamiltonian, density, ham_pattern.T, den_pattern, tile_basis, offsets)


def solution(mesh):
    in_specs = (
        P("row", ("rep", "col")),
        P(("rep", "row"), "col"),
        P("row", ("rep", "col")),
        P(("rep", "row"), "col"),
        P(None, None, "col"),
        P(("row", "rep")),
    )
    out_specs = (P(("row", "rep"), "col"), P(("row", "rep"), "col"))
    body = functools.partial(shards, mesh.shape["row"], mesh.shape["col"])
    return jax.shard_map(body, mesh=mesh, in_specs=in_specs, out_specs=out_specs, check_vma=False)
```
